256 devices in a mesh: tok: 32 (over x, y, core), head: 8 (over z).
Axes of the slice: x: 4, y: 4, z: 8, core: 2. Of those that a mesh axis runs over, the one named last changes fastest.
Arguments:
- queries: bfloat16 [8192, 8192], P(('tok', 'head')), may hold values from -5 to 5, as said below
- key_rows: bfloat16 [8192, 1024], P(('tok', 'head')), may hold values from -5 to 5, as said below
- value_rows: bfloat16 [8192, 1024], P(('tok', 'head')), may hold values from -5 to 5
- out_grad: bfloat16 [8192, 8192], P(('tok', 'head')), may hold values from -5 to 5
- lengths: int32 [8], replicated, may hold values from 1 to 2048, 8192 in all
- server_plan: int32 [1024], replicated, may hold values from 0 to 1023, as said below
Outputs:
- attended: bfloat16 [8192, 8192], P('tok', 'head')
- grad_query: bfloat16 [8192, 8192], P('tok', 'head')
- grad_key: bfloat16 [8192, 1024], P('tok', 'head')
- grad_value: bfloat16 [8192, 1024], P('tok', 'head')
- served_logsum: float32 [64, 8192], P('head', 'tok')
The draws below stay inside these ranges and needn't reach their ends.
Inputs may be any that keep to these rules, and one draw needn't show every extreme that they name: `lengths`: the longest trajectory has exactly 2048 tokens. `server_plan`: a permutation of the 1024 query pieces (piece p holds tokens p * 8 to p * 8 + 7 and belongs to owner p // 32); server s holds entries s * 32 to s * 32 + 31; every server holds exactly one piece of every owner. `queries`: entries of order one. `key_rows`: entries of order one.
All inputs are finite; a program needn't handle non-finite values.
Results may differ from the reference program's by a relative error of at most 0.012.
Values may be sent and summed in bfloat16 or wider, within the bound.
A program may use at most 64 MiB of HBM per device.

```python
import math
import jax
import jax.numpy as jnp
import numpy as np
from jax import lax

QH = 64
KVH = 8
HD = 128
PIECE = 8
TOKENS = 8192
MOST = 2048
NTRAJ = 8
NPIECE = 1024
SLOTS = 32


def draw_queries(key, part):
    key = jax.random.fold_in(key, 11)
    base = jnp.clip(jax.random.normal(key, (TOKENS, QH * HD), jnp.float32), -5.0, 5.0)
    return base.astype(jnp.bfloat16)


def draw_key_rows(key, part):
    key = jax.random.fold_in(key, 17)
    base = jnp.clip(jax.random.normal(key, (TOKENS, KVH * HD), jnp.float32), -5.0, 5.0)
    return base.astype(jnp.bfloat16)


def draw_server_plan(key, part):
    key = jax.random.fold_in(key, 23)
    owner_key, offset_key, order_key = jax.random.split(key, 3)
    servers = NPIECE // SLOTS
    owner_perm = jax.random.permutation(owner_key, servers)
    offsets = jax.random.permutation(offset_key, servers)[:SLOTS]
    server_ids = jnp.arange(servers, dtype=jnp.int32)
    based = (server_ids[:, None] - offsets[None, :]) % servers
    inverse = jnp.argsort(owner_perm)
    owner = inverse[based]
    piece = owner * SLOTS + jnp.arange(SLOTS, dtype=jnp.int32)[None, :]
    orders = jax.vmap(lambda sub: jax.random.permutation(sub, SLOTS))(jax.random.split(order_key, servers))
    placed = jnp.zeros((servers, SLOTS), jnp.int32).at[server_ids[:, None], orders].set(piece.astype(jnp.int32))
    return placed.reshape(servers * SLOTS).astype(jnp.int32)


def block_scale(own_key, shape, shards, smallest, high):
    loudness, own = 1.0, jax.random.fold_in(own_key, 6)
    for axis_at, blocks in shards:
        heights = jnp.exp(jax.random.uniform(jax.random.fold_in(own, axis_at), (blocks,), jnp.float32, smallest / len(shards), high / len(shards)))
        loudness = loudness * jnp.repeat(heights, shape[axis_at] // blocks).reshape([-1 if axis == axis_at else 1 for axis in range(len(shape))])
    return loudness


def split_up(amount, total, bound, slope):
    loads = [(1 << 20) // math.isqrt(rank ** slope) + 1 for rank in range(2, amount + 1)]
    spare, counts = total - bound - (amount - 1), [1] * (amount - 1)
    while spare > 0:
        movable = [i for i in range(amount - 1) if counts[i] < bound]
        whole, budget = sum([loads[i] for i in movable]), spare
        for i in movable:
            extra = min(bound - counts[i], max(1, budget * loads[i] // whole), spare)
            counts[i] = counts[i] + extra
            spare = spare - extra
    return np.array([bound] + counts)


def uneven(key, number_of, total, bound, lean):
    if number_of == 2:
        one = jax.random.randint(key, (), max(1, total - bound), min(bound, total - 1) + 1)
        return jnp.stack([one, total - one])
    tallies = jnp.asarray(split_up(number_of, total, bound, lean), jnp.int32)
    twos = (number_of - 1) // 2
    giver, sink = tallies[1:1 + 2 * twos:2], tallies[2:2 + 2 * twos:2]
    room = jnp.minimum(giver - 1, bound - sink)
    shifted = jax.random.randint(jax.random.fold_in(key, 1), (twos,), 0, 1 << 20) % (room + 1)
    tallies = tallies.at[1:1 + 2 * twos:2].set(giver - shifted).at[2:2 + 2 * twos:2].set(sink + shifted)
    return tallies[jax.random.permutation(jax.random.fold_in(key, 2), number_of)]


def bell_draw(stream_key, dims, scale, reach, shards=(), held_as=jnp.bfloat16):
    drawn = scale * jax.random.normal(stream_key, dims, jnp.float32)
    if shards:
        drawn = drawn * block_scale(stream_key, dims, shards, -0.22, 0.18)
    return jnp.clip(drawn, -reach, reach).astype(held_as)


def setup_inputs(seed: int = 0) -> dict:
    seeds = jax.random.split(jax.random.key(seed), 7)
    queries = draw_queries(jax.random.fold_in(seeds[6], 71), 0)
    key_rows = draw_key_rows(jax.random.fold_in(seeds[6], 71), 0)
    value_rows = bell_draw(seeds[2], (TOKENS, KVH * HD), 1.0, 5.0, ((0, 256),))
    out_grad = bell_draw(seeds[3], (TOKENS, QH * HD), 1.0, 5.0, ((0, 256),))
    lengths = uneven(seeds[4], NTRAJ, TOKENS, MOST, 2).astype(jnp.int32)
    server_plan = draw_server_plan(jax.random.fold_in(seeds[6], 71), 0)
    return {"queries": queries, "key_rows": key_rows, "value_rows": value_rows, "out_grad": out_grad, "lengths": lengths, "server_plan": server_plan}


masked_fill = -1e30


def segment_ids(lengths, count):
    ends = jnp.cumsum(lengths)
    position = jnp.arange(count, dtype=jnp.int32)
    return jnp.sum((ends[None, :] <= position[:, None]).astype(jnp.int32), axis=1)


def widened(form, left, right):
    return jnp.einsum(form, left.astype(jnp.float32), right.astype(jnp.float32))


def one_piece(query_block, grad_block, offset, gathered, trajectory, window_len):
    row_count = query_block.shape[0]
    kv_heads = gathered.shape[1] // (2 * HD)
    group_size = query_block.shape[1] // (kv_heads * HD)
    whole = gathered.shape[0]
    wstart = jnp.clip(offset + row_count - window_len, 0, whole - window_len).astype(jnp.int32)
    window = lax.dynamic_slice_in_dim(gathered, wstart, window_len, 0)
    key_block = window[:, :kv_heads * HD].reshape(window_len, kv_heads, HD)
    value_block = window[:, kv_heads * HD:].reshape(window_len, kv_heads, HD)
    query = query_block.reshape(row_count, kv_heads, group_size, HD)
    upstream = grad_block.reshape(row_count, kv_heads, group_size, HD)
    query_pos = offset + jnp.arange(row_count, dtype=jnp.int32)
    key_pos = wstart + jnp.arange(window_len, dtype=jnp.int32)
    query_seg = lax.dynamic_slice_in_dim(trajectory, offset, row_count, 0)
    key_seg = lax.dynamic_slice_in_dim(trajectory, wstart, window_len, 0)
    allowed = (query_seg[:, None] == key_seg[None, :]) & (key_pos[None, :] <= query_pos[:, None])
    inv_root = HD ** -0.5
    scores = widened("rkgd,mkd->kgrm", query, key_block) * inv_root
    scores = jnp.where(allowed[None, None], scores, masked_fill)
    row_max = jnp.max(scores, axis=-1, keepdims=True)
    raised = jnp.exp(scores - row_max)
    summed = jnp.sum(raised, axis=-1, keepdims=True)
    weights = raised / summed
    log_total = (row_max + jnp.log(summed))[..., 0]
    weights_low = lax.optimization_barrier(weights.astype(jnp.bfloat16))
    attended = widened("kgrm,mkd->rkgd", weights_low, value_block)
    attended_low = lax.optimization_barrier(attended.astype(jnp.bfloat16))
    out_dot = jnp.sum(upstream.astype(jnp.float32) * attended_low.astype(jnp.float32), axis=-1)
    grad_weight = widened("rkgd,mkd->kgrm", upstream, value_block)
    dscore = weights * (grad_weight - jnp.transpose(out_dot, (1, 2, 0))[..., None])
    dscore_low = lax.optimization_barrier(dscore.astype(jnp.bfloat16))
    dquery = widened("kgrm,mkd->rkgd", dscore_low, key_block) * inv_root
    grad_keys = widened("kgrm,rkgd->mkd", dscore_low, query) * inv_root
    grad_values = widened("kgrm,rkgd->mkd", weights_low, upstream)
    window_grad = jnp.concatenate([grad_keys.reshape(window_len, kv_heads * HD), grad_values.reshape(window_len, kv_heads * HD)], axis=1)
    return attended_low.reshape(row_count, -1), dquery.astype(jnp.bfloat16).reshape(row_count, -1), log_total, wstart, window_grad


def serve_all(query_pieces, grad_pieces, offsets, gathered, trajectory, window_len):
    def advance(grad_total, inputs):
        query_block, grad_block, offset = inputs
        attended, dquery, log_total, wstart, window_grad = one_piece(query_block, grad_block, offset, gathered, trajectory, window_len)
        previous = lax.dynamic_slice_in_dim(grad_total, wstart, window_len, 0)
        grad_total = lax.dynamic_update_slice_in_dim(grad_total, previous + window_grad, wstart, 0)
        return grad_total, (attended, dquery, log_total)

    initial = jnp.zeros((gathered.shape[0], gathered.shape[1]), jnp.float32)
    return lax.scan(advance, initial, (query_pieces, grad_pieces, offsets))


def reference(queries, key_rows, value_rows, out_grad, lengths, server_plan):
    trajectory = segment_ids(lengths, TOKENS)
    gathered = jnp.concatenate([key_rows, value_rows], axis=1)
    query_pieces = queries.reshape(NPIECE, PIECE, QH * HD)
    grad_pieces = out_grad.reshape(NPIECE, PIECE, QH * HD)
    offsets = jnp.arange(NPIECE, dtype=jnp.int32) * PIECE
    grad_total, (attended, dquery, log_total) = serve_all(query_pieces, grad_pieces, offsets, gathered, trajectory, MOST)
    attended_rows = attended.reshape(TOKENS, QH * HD)
    dquery_rows = dquery.reshape(TOKENS, QH * HD)
    grad_key = grad_total[:, :KVH * HD].astype(jnp.bfloat16)
    grad_value = grad_total[:, KVH * HD:].astype(jnp.bfloat16)
    log_pieces = log_total.reshape(NPIECE, QH, PIECE)
    served_log = jnp.take(log_pieces, server_plan.astype(jnp.int32), axis=0)
    served_logsum = jnp.transpose(served_log, (1, 0, 2)).reshape(QH, TOKENS)
    return (attended_rows, dquery_rows, grad_key, grad_value, served_logsum)
```

```python
import functools

import jax
import jax.numpy as jnp
from jax import lax
from jax.experimental import pallas as pl
from jax.experimental.pallas import tpu as pltpu
from jax.sharding import PartitionSpec as P

bf16, f32, i32 = jnp.bfloat16, jnp.float32, jnp.int32
HD = 128
T = 256
NW = 9
NT_ = 32
NH = 8
RB = T // NH
NCH = 4
NTRAJ = 8
SCALE = HD**-0.5
LOG2E = 1.4426950408889634
C = SCALE * LOG2E
BIG = 1e30
MESH = pl.DeviceIdType.MESH

NN, NT = ((1,), (0,)), ((1,), (1,))


def dot(a, b, dims):
    return lax.dot_general(a, b, (dims, ((), ())), preferred_element_type=f32)


def fwd_head(q, kv, maskq, maskk, s_scr, p_scr):
    qa = jnp.concatenate([q, maskq], axis=1)
    mx = None
    for w in range(NW):
        ka = jnp.concatenate([kv[w, :, :HD], maskk[w]], axis=1)
        s = dot(qa, ka, NT)
        if w == NW - 1:
            r = lax.broadcasted_iota(i32, (T, T), 0)
            c = lax.broadcasted_iota(i32, (T, T), 1)
            s = jnp.where(c <= r, s, -BIG)
        s_scr[:, w * T : (w + 1) * T] = s
        m2 = jnp.maximum(s[:, :HD], s[:, HD:])
        mx = m2 if mx is None else jnp.maximum(mx, m2)
    m = jnp.max(mx, axis=1, keepdims=True)
    acc = jnp.zeros((T, T), f32)
    ones = jnp.ones((T, HD), bf16)
    for w in range(NW):
        p = jnp.exp2((s_scr[:, w * T : (w + 1) * T] - m) * C).astype(bf16)
        p_scr[:, w * T : (w + 1) * T] = p
        va = jnp.concatenate([kv[w, :, HD:], ones], axis=1)
        acc = acc + dot(p, va, NN)
    l = acc[:, HD:]
    li = 1.0 / l
    att = (acc[:, :HD] * li).astype(bf16)
    return att, li, m * SCALE + jnp.log(l)


def bwd_head(q, do, kv, p_scr, att, li, dkv_t):
    dof = do.astype(f32)
    neg = -jnp.sum(dof * att.astype(f32), axis=1, keepdims=True)
    d1 = neg.astype(bf16).astype(f32)
    d2 = (neg - d1).astype(bf16).astype(f32)
    d3 = neg - d1 - d2
    lane = lax.broadcasted_iota(i32, (T, HD), 1)
    ext = jnp.where(
        lane == 0, d1, jnp.where(lane == 1, d2, jnp.where(lane == 2, d3, 0.0))
    ).astype(bf16)
    doa = jnp.concatenate([do, ext], axis=1)
    q_t = (q.astype(f32) * li * SCALE).astype(bf16).T
    do_t = (dof * li).astype(bf16).T
    ones = jnp.ones((T, HD), bf16)
    acc = jnp.zeros((T, HD), f32)
    for w in range(NW):
        p = p_scr[:, w * T : (w + 1) * T]
        va = jnp.concatenate([kv[w, :, HD:], ones], axis=1)
        ds = (p.astype(f32) * dot(doa, va, NT)).astype(bf16)
        acc = acc + dot(ds, kv[w, :, :HD], NN)
        dkv_t[w, :HD, :] += dot(q_t, ds, NN)
        dkv_t[w, HD:, :] += dot(do_t, p, NN)
    return (acc * li * SCALE).astype(bf16)


def kernel(
    q_in, k_in, v_in, do_in, lengths, plan,
    att_out, dq_out, dk_out, dv_out, ls_out,
    qbuf, dobuf, kv, maskq, maskk, s_scr, p_all, linv, lcol, lsend, lall, dkv_t, gsend, grecv,
    own_sem, z_send, kv_recv, q_recv, do_recv, w_send, w_recv, l_send, l_recv, g_send, g_recv,
):
    me_t, me_h = lax.axis_index("tok"), lax.axis_index("head")

    def tok_peer(d):
        return (lax.rem(me_t + d, NT_), me_h)

    def head_peer(d):
        return (me_t, lax.rem(me_h + d, NH))

    barrier = pltpu.get_barrier_semaphore()
    for d in range(1, NH):
        pl.semaphore_signal(barrier, inc=1, device_id=head_peer(d), device_id_type=MESH)

    @pl.loop(1, NT_)
    def _(d):
        pl.semaphore_signal(barrier, inc=1, device_id=tok_peer(d), device_id_type=MESH)

    pl.semaphore_wait(barrier, NH - 1 + NT_ - 1)

    rows = pl.ds(pl.multiple_of(me_h * RB, RB), RB)

    def remote(src, dst, send, recv, peer):
        return pltpu.make_async_remote_copy(
            src_ref=src, dst_ref=dst, send_sem=send, recv_sem=recv,
            device_id=peer, device_id_type=MESH,
        )

    def z_sends(d):
        h = lax.rem(me_h + d, NH)
        peer = (me_t, h)
        cols = pl.ds(pl.multiple_of(h * HD, HD), HD)
        remote(k_in.at[:, cols], kv.at[NW - 1, rows, :HD], z_send.at[0], kv_recv, peer).start()
        remote(v_in.at[:, cols], kv.at[NW - 1, rows, HD:], z_send.at[0], kv_recv, peer).start()

    def big_sends(src, buf, send, recv):
        for c in range(NCH):
            for d in range(1, NH):
                h = lax.rem(me_h + d, NH)
                cols = pl.ds(pl.multiple_of(h * NH * HD + c * T, T), T)
                remote(src.at[:, cols], buf.at[c, rows], send, recv.at[c], (me_t, h)).start()

    for d in range(1, NH):
        z_sends(d)
    big_sends(q_in, qbuf, z_send.at[1], q_recv)
    big_sends(do_in, dobuf, z_send.at[2], do_recv)

    own_cols = pl.ds(pl.multiple_of(me_h * HD, HD), HD)
    own = [
        (k_in.at[:, own_cols], kv.at[NW - 1, rows, :HD]),
        (v_in.at[:, own_cols], kv.at[NW - 1, rows, HD:]),
    ]
    for c in range(NCH):
        cols = pl.ds(pl.multiple_of(me_h * NH * HD + c * T, T), T)
        own.append((q_in.at[:, cols], qbuf.at[c, rows]))
        own.append((do_in.at[:, cols], dobuf.at[c, rows]))
    own = [pltpu.make_async_copy(s, t, own_sem.at[i]) for i, (s, t) in enumerate(own)]
    for copy in own:
        copy.start()

    lane = lax.broadcasted_iota(i32, (1, HD), 1)
    first = jnp.zeros((1, HD), i32)
    last = jnp.zeros((1, HD), i32)
    run = jnp.int32(0)
    for n in range(NTRAJ):
        first = jnp.where(lane == n, run, first)
        run = run + lengths[n]
        last = jnp.where(lane == n, run, last)
    row = lax.broadcasted_iota(i32, (T, HD), 0)
    for w in range(NW):
        pos = row + (me_t + w - (NW - 1)) * T
        inside = (pos >= first) & (pos < last)
        maskk[w] = jnp.where(inside, 0.0, 1.0).astype(bf16)
        if w == NW - 1:
            maskq[...] = jnp.where(inside, -BIG, 0.0).astype(bf16)
        dkv_t[w] = jnp.zeros((T, T), f32)
    lcol[...] = jnp.zeros((T, HD), f32)

    def all_bytes(ref, sem):
        pltpu.make_async_copy(ref, ref, sem).wait()

    for copy in own:
        copy.wait()
    all_bytes(kv.at[NW - 1, : T - RB], kv_recv)

    for d in range(1, NW):
        remote(kv.at[NW - 1], kv.at[NW - 1 - d], w_send, w_recv.at[d - 1], tok_peer(d)).start()
    for d in range(1, NW):
        all_bytes(kv.at[NW - 1 - d], w_recv.at[d - 1])

    @pl.loop(0, NCH)
    def _(c):
        all_bytes(qbuf.at[c, : T - RB], q_recv.at[c])
        for i in range(2):
            j = 2 * c + i
            att, li, ls = fwd_head(
                qbuf[c, :, i * HD : (i + 1) * HD], kv, maskq[...], maskk, s_scr, p_all.at[j]
            )
            linv[j] = li
            att_out[:, pl.ds(pl.multiple_of(j * HD, HD), HD)] = att
            lanes = lax.broadcasted_iota(i32, (T, HD), 1)
            lcol[...] = jnp.where(lanes == j, ls, lcol[...])

    flat = lcol[...].T[:NH]
    lsend[0] = flat[:, :HD]
    lsend[1] = flat[:, HD:]

    @pl.loop(1, NT_)
    def _(d):
        remote(lsend, lall.at[me_t], l_send, l_recv, tok_peer(d)).start()

    lall[me_t] = lsend[...]

    @pl.loop(0, NCH)
    def _(c):
        all_bytes(dobuf.at[c, : T - RB], do_recv.at[c])
        for i in range(2):
            j = 2 * c + i
            at = pl.ds(pl.multiple_of(j * HD, HD), HD)
            half = slice(i * HD, (i + 1) * HD)
            dq_out[:, at] = bwd_head(
                qbuf[c, :, half], dobuf[c, :, half], kv, p_all.at[j], att_out[:, at], linv[j], dkv_t
            )

    for w in range(NW - 1):
        gsend[w] = dkv_t[w].astype(bf16)
        remote(
            gsend.at[w], grecv.at[w], g_send, g_recv.at[w], tok_peer(NT_ - (NW - 1 - w))
        ).start()

    all_bytes(lall.at[: NT_ - 1], l_recv)
    lane = lax.broadcasted_iota(i32, (NH, HD), 1)
    for half in range(2):
        picked = jnp.zeros((NH, HD), f32)
        for n in range(16):
            piece = plan[me_t * 32 + half * 16 + n]
            owner, local = piece // 32, lax.rem(piece, 32)
            tile = lall[owner, local // 16]
            shift = lax.rem(8 * n - 8 * lax.rem(local, 16) + HD, HD)
            picked = jnp.where(lane // 8 == n, pltpu.roll(tile, shift, 1), picked)
        ls_out[:, half * HD : (half + 1) * HD] = picked

    total = dkv_t[NW - 1]
    for w in range(NW - 1):
        all_bytes(grecv.at[w], g_recv.at[w])
        total = total + grecv[w].astype(f32)
    dk_out[...] = total[:HD].T.astype(bf16)
    dv_out[...] = total[HD:].T.astype(bf16)

    all_bytes(kv.at[NW - 1, : T - RB], z_send.at[0])
    all_bytes(qbuf.at[:, : T - RB], z_send.at[1])
    all_bytes(dobuf.at[:, : T - RB], z_send.at[2])
    all_bytes(kv.at[: NW - 1], w_send)
    all_bytes(lall.at[: NT_ - 1], l_send)
    all_bytes(gsend, g_send)


def body(queries, key_rows, value_rows, out_grad, lengths, server_plan):
    any_spec = pl.BlockSpec(memory_space=pl.ANY)
    vmem = pl.BlockSpec(memory_space=pltpu.VMEM)
    smem = pl.BlockSpec(memory_space=pltpu.SMEM)
    dma, V = pltpu.SemaphoreType.DMA, pltpu.VMEM
    return pl.pallas_call(
        kernel,
        out_shape=[
            jax.ShapeDtypeStruct((T, NH * HD), bf16),
            jax.ShapeDtypeStruct((T, NH * HD), bf16),
            jax.ShapeDtypeStruct((T, HD), bf16),
            jax.ShapeDtypeStruct((T, HD), bf16),
            jax.ShapeDtypeStruct((NH, T), f32),
        ],
        in_specs=[any_spec] * 4 + [smem] * 2,
        out_specs=[vmem] * 5,
        scratch_shapes=[
            V((NCH, T, T), bf16),
            V((NCH, T, T), bf16),
            V((NW, T, 2 * HD), bf16),
            V((T, HD), bf16),
            V((NW, T, HD), bf16),
            V((T, NW * T), f32),
            V((NH, T, NW * T), bf16),
            V((NH, T, HD), f32),
            V((T, HD), f32),
            V((2, NH, HD), f32),
            V((NT_, 2, NH, HD), f32),
            V((NW, T, T), f32),
            V((NW - 1, T, T), bf16),
            V((NW - 1, T, T), bf16),
            dma((2 + 2 * NCH,)),
            dma((3,)),
            dma(()),
            dma((NCH,)),
            dma((NCH,)),
            dma(()),
            dma((NW - 1,)),
            dma(()),
            dma(()),
            dma(()),
            dma((NW - 1,)),
        ],
        compiler_params=pltpu.CompilerParams(
            collective_id=0, has_side_effects=True, vmem_limit_bytes=56 * 2**20
        ),
        cost_estimate=pl.CostEstimate(
            flops=8 * 10**9, bytes_accessed=6 * 2**20, transcendentals=5 * 10**6
        ),
        name="attention",
    )(queries, key_rows, value_rows, out_grad, lengths, server_plan)


def solution(mesh):
    in_specs = (
        P(("tok", "head"), None),
        P(("tok", "head"), None),
        P(("tok", "head"), None),
        P(("tok", "head"), None),
        P(),
        P(),
    )
    out_specs = (
        P("tok", "head"),
        P("tok", "head"),
        P("tok", "head"),
        P("tok", "head"),
        P("head", "tok"),
    )
    return jax.shard_map(body, mesh=mesh, in_specs=in_specs, out_specs=out_specs, check_vma=False)
```

```python
import functools

import jax
import jax.numpy as jnp
from jax import lax
from jax.experimental import pallas as pl
from jax.experimental.pallas import tpu as pltpu
from jax.sharding import PartitionSpec as P

bf16, f32, i32 = jnp.bfloat16, jnp.float32, jnp.int32
HD = 128
T = 256
NW = 9
NT_ = 32
NH = 8
RB = T // NH
NCH = 4
GR = 4 * T
NY = 4
NTRAJ = 8
SCALE = HD**-0.5
LOG2E = 1.4426950408889634
C = SCALE * LOG2E
BIG = 1e30
MESH = pl.DeviceIdType.MESH

NN, NT = ((1,), (0,)), ((1,), (1,))


def dot(a, b, dims):
    return lax.dot_general(a, b, (dims, ((), ())), preferred_element_type=f32)


def rows_of(buf, c):
    return jnp.concatenate([buf[c, :, :HD], buf[c, :, HD:]], axis=0)


def group_of(buf, g):
    return jnp.concatenate([rows_of(buf, 2 * g), rows_of(buf, 2 * g + 1)], axis=0)


def scores(w, c, qbuf, kv, maskq, maskk, s_all, mx):
    q = rows_of(qbuf, c)
    mask = maskq[...]
    qa = jnp.concatenate([q, jnp.concatenate([mask, mask], axis=0)], axis=1)
    ka = jnp.concatenate([kv[w, 0], maskk[w]], axis=1)
    s = dot(qa, ka, NT)
    if w == NW - 1:
        r = lax.rem(lax.broadcasted_iota(i32, s.shape, 0), T)
        s = jnp.where(lax.broadcasted_iota(i32, s.shape, 1) <= r, s, -BIG)
    at = pl.ds(pl.multiple_of(c * 2 * T, 2 * T), 2 * T)
    s_all[at, w * T : (w + 1) * T] = s
    m = jnp.maximum(s[:, :HD], s[:, HD:])
    mx[at] = m if w == NW - 1 else jnp.maximum(mx[at], m)


def softmax(at, kv, s_all, mx, p_all):
    m = jnp.max(mx[at], axis=1, keepdims=True) * C
    acc = jnp.zeros((GR, 2 * HD), f32)
    ones = jnp.ones((T, HD), bf16)
    for w in range(NW):
        p = jnp.exp2(s_all[at, w * T : (w + 1) * T] * C - m).astype(bf16)
        p_all[at, w * T : (w + 1) * T] = p
        acc = acc + dot(p, jnp.concatenate([kv[w, 1], ones], axis=1), NN)
    l = acc[:, HD:]
    li = 1.0 / l
    return (acc[:, :HD] * li).astype(bf16), li, m * (1.0 / LOG2E) + jnp.log(l)


def with_out_dot(do, att):
    neg = -jnp.sum(do.astype(f32) * att.astype(f32), axis=1, keepdims=True)
    d1 = neg.astype(bf16).astype(f32)
    d2 = (neg - d1).astype(bf16).astype(f32)
    d3 = neg - d1 - d2
    lane = lax.broadcasted_iota(i32, do.shape, 1)
    ext = jnp.where(
        lane == 0, d1, jnp.where(lane == 1, d2, jnp.where(lane == 2, d3, 0.0))
    ).astype(bf16)
    return jnp.concatenate([do, ext], axis=1)


def kernel(
    q_in, k_in, v_in, do_in, lengths, plan,
    att_out, dq_out, dk_out, dv_out, ls_out,
    qbuf, dobuf, kv, maskq, maskk, s_all, mx, p_all, att, linv, lcol, lsend, lall, dkv_t,
    gs_out, gs_in, gy_out, gy_in, gx_out, gx_in,
    own_sem, z_send, kv_recv, q_recv, do_recv, w_send, wx_recv, wy_recv, ws_recv, l_send, l_recv,
    g_send, gs_recv, gy_recv, gx_recv,
):
    me_t, me_h = lax.axis_index("tok"), lax.axis_index("head")

    core = lax.rem(me_t, 2)
    y = lax.rem(me_t // 2, NY)
    x_up = (lax.rem(me_t + 2 * NY, NT_), me_h)
    x_down = (lax.rem(me_t + NT_ - 2 * NY, NT_), me_h)
    sibling = (me_t + 1 - 2 * core, me_h)

    def y_peer(d):
        return (me_t + 2 * (lax.rem(y + d, NY) - y), me_h)

    def tok_peer(d):
        return (lax.rem(me_t + d, NT_), me_h)

    def head_peer(d):
        return (me_t, lax.rem(me_h + d, NH))

    barrier = pltpu.get_barrier_semaphore()
    for d in range(1, NH):
        pl.semaphore_signal(barrier, inc=1, device_id=head_peer(d), device_id_type=MESH)

    @pl.loop(1, NT_)
    def _(d):
        pl.semaphore_signal(barrier, inc=1, device_id=tok_peer(d), device_id_type=MESH)

    pl.semaphore_wait(barrier, NH - 1 + NT_ - 1)

    rows = pl.ds(pl.multiple_of(me_h * RB, RB), RB)

    def remote(src, dst, send, recv, peer):
        return pltpu.make_async_remote_copy(
            src_ref=src, dst_ref=dst, send_sem=send, recv_sem=recv,
            device_id=peer, device_id_type=MESH,
        )

    def z_sends(d):
        h = lax.rem(me_h + d, NH)
        peer = (me_t, h)
        cols = pl.ds(pl.multiple_of(h * HD, HD), HD)
        remote(k_in.at[:, cols], kv.at[NW - 1, 0, rows], z_send.at[0], kv_recv, peer).start()
        remote(v_in.at[:, cols], kv.at[NW - 1, 1, rows], z_send.at[0], kv_recv, peer).start()

    def big_sends(src, buf, send, recv):
        for c in range(NCH):
            for d in range(1, NH):
                h = lax.rem(me_h + d, NH)
                cols = pl.ds(pl.multiple_of(h * NH * HD + c * T, T), T)
                remote(src.at[:, cols], buf.at[c, rows], send, recv.at[c], (me_t, h)).start()

    for d in range(1, NH):
        z_sends(d)
    big_sends(q_in, qbuf, z_send.at[1], q_recv)
    big_sends(do_in, dobuf, z_send.at[2], do_recv)

    own_cols = pl.ds(pl.multiple_of(me_h * HD, HD), HD)
    own = [
        (k_in.at[:, own_cols], kv.at[NW - 1, 0, rows]),
        (v_in.at[:, own_cols], kv.at[NW - 1, 1, rows]),
    ]
    for c in range(NCH):
        cols = pl.ds(pl.multiple_of(me_h * NH * HD + c * T, T), T)
        own.append((q_in.at[:, cols], qbuf.at[c, rows]))
        own.append((do_in.at[:, cols], dobuf.at[c, rows]))
    own = [pltpu.make_async_copy(s, t, own_sem.at[i]) for i, (s, t) in enumerate(own)]
    for copy in own:
        copy.start()

    lane = lax.broadcasted_iota(i32, (1, HD), 1)
    first = jnp.zeros((1, HD), i32)
    last = jnp.zeros((1, HD), i32)
    run = jnp.int32(0)
    for n in range(NTRAJ):
        first = jnp.where(lane == n, run, first)
        run = run + lengths[n]
        last = jnp.where(lane == n, run, last)
    row = lax.broadcasted_iota(i32, (T, HD), 0)
    for w in range(NW):
        pos = row + (me_t + w - (NW - 1)) * T
        inside = (pos >= first) & (pos < last)
        maskk[w] = jnp.where(inside, 0.0, 1.0).astype(bf16)
        if w == NW - 1:
            maskq[...] = jnp.where(inside, -BIG, 0.0).astype(bf16)
    lcol[...] = jnp.zeros((T, HD), f32)

    def all_bytes(ref, sem):
        pltpu.make_async_copy(ref, ref, sem).wait()

    for copy in own:
        copy.wait()
    all_bytes(kv.at[NW - 1, :, : T - RB], kv_recv)

    def window(src, dst, recv, peer):
        remote(kv.at[src], kv.at[dst], w_send, recv, peer).start()

    def share(d):
        i = d - core
        window(8 - 2 * d, 7 - 2 * i, ws_recv.at[i], sibling)

    window(8, 0, wx_recv, x_up)
    for d in (1, 3, 2):
        pl.when(y + d < NY)(lambda d=d: window(8, 8 - 2 * d, wy_recv.at[d - 1], y_peer(d)))
    pl.when(core == 0)(lambda: share(0))
    all_bytes(kv.at[0], wx_recv)
    for d in (1, 3, 2):
        pl.when(y + d >= NY)(lambda d=d: window(0, 8 - 2 * d, wy_recv.at[d - 1], y_peer(d)))
    pl.when(core == 1)(lambda: share(4))
    for d in (1, 3, 2):
        all_bytes(kv.at[8 - 2 * d], wy_recv.at[d - 1])
        share(d)

    for w in (8, 0, 6, 4, 2, 7, 5, 3, 1):
        if w % 2:
            all_bytes(kv.at[w], ws_recv.at[(7 - w) // 2])

        @pl.loop(0, NCH)
        def _(c):
            if w == NW - 1:
                all_bytes(qbuf.at[c, : T - RB], q_recv.at[c])
            scores(w, c, qbuf, kv, maskq, maskk, s_all, mx)

    @pl.loop(0, 2)
    def _(g):
        at = pl.ds(pl.multiple_of(g * GR, GR), GR)
        out, li, ls = softmax(at, kv, s_all, mx, p_all)
        att[at] = out
        linv[at] = li
        lanes = lax.broadcasted_iota(i32, (T, HD), 1)
        col = lcol[...]
        for i in range(4):
            col = jnp.where(lanes == 4 * g + i, ls[i * T : (i + 1) * T], col)
            att_out[:, pl.ds(pl.multiple_of((4 * g + i) * HD, HD), HD)] = out[i * T : (i + 1) * T]
        lcol[...] = col

    flat = lcol[...].T[:NH]
    lsend[0] = flat[:, :HD]
    lsend[1] = flat[:, HD:]

    @pl.loop(1, NT_)
    def _(d):
        remote(lsend, lall.at[me_t], l_send, l_recv, tok_peer(d)).start()

    lall[me_t] = lsend[...]

    def sib_send(p, i):
        gs_out[p, i] = dkv_t[p, 7 - 2 * i].astype(bf16)
        remote(gs_out.at[p, i], gs_in.at[p, i], g_send.at[0], gs_recv.at[p, i], sibling).start()

    def y_send(p, d):
        i = d - core
        all_bytes(gs_in.at[p, i], gs_recv.at[p, i])
        gy_out[p, d - 1] = (dkv_t[p, 8 - 2 * d] + gs_in[p, i].astype(f32)).astype(bf16)
        remote(
            gy_out.at[p, d - 1], gy_in.at[p, d - 1], g_send.at[1], gy_recv.at[p, d - 1], y_peer(NY - d)
        ).start()

    def only(cond, ref):
        return jnp.where(cond, ref.astype(f32), 0.0)

    def x_send(p):
        all_bytes(gs_in.at[p, 3 * core], gs_recv.at[p, 3 * core])
        total = dkv_t[p, 0] + only(core == 1, gs_in[p, 3 * core])
        for d in (1, 2, 3):
            all_bytes(gy_in.at[p, d - 1], gy_recv.at[p, d - 1])
            total = total + only(y + d >= NY, gy_in[p, d - 1])
        gx_out[p] = total.astype(bf16)
        remote(gx_out.at[p], gx_in.at[p], g_send.at[2], gx_recv.at[p], x_down).start()

    def summed(p):
        total = dkv_t[p, 8] + only(core == 0, gs_in[p, 3 * core])
        for d in (1, 2, 3):
            total = total + only(y + d < NY, gy_in[p, d - 1])
        all_bytes(gx_in.at[p], gx_recv.at[p])
        return (total + gx_in[p].astype(f32)).T.astype(bf16)

    def passed_on(p, w):
        if w % 2:
            sib_send(p, (7 - w) // 2)
        elif w not in (0, 8):
            y_send(p, (8 - w) // 2)

    order = (7, 5, 6, 3, 4, 1, 2, 0, 8)
    ones = jnp.ones((T, HD), bf16)
    for g in range(2):
        at = slice(g * GR, (g + 1) * GR)
        for c in (2 * g, 2 * g + 1):
            all_bytes(dobuf.at[c, : T - RB], do_recv.at[c])
        do = group_of(dobuf, g)
        li = linv[at]
        do_t = (do.astype(f32) * li).astype(bf16).T
        q_t = (group_of(qbuf, g).astype(f32) * li * SCALE).astype(bf16).T
        doa = with_out_dot(do, att[at])
        for w in order:
            dv = dot(do_t, p_all[at, w * T : (w + 1) * T], NN)
            if g == 0:
                dkv_t[1, w] = dv
            else:
                dkv_t[1, w] += dv
                passed_on(1, w)
        acc = jnp.zeros((GR, HD), f32)
        for w in order:
            p = p_all[at, w * T : (w + 1) * T]
            va = jnp.concatenate([kv[w, 1], ones], axis=1)
            ds = (p.astype(f32) * dot(doa, va, NT)).astype(bf16)
            acc = acc + dot(ds, kv[w, 0], NN)
            dk = dot(q_t, ds, NN)
            if g == 0:
                dkv_t[0, w] = dk
            else:
                dkv_t[0, w] += dk
                passed_on(0, w)
        dq = (acc * li * SCALE).astype(bf16)
        for i in range(4):
            dq_out[:, (4 * g + i) * HD : (4 * g + i + 1) * HD] = dq[i * T : (i + 1) * T]
    x_send(1)
    x_send(0)

    all_bytes(lall.at[: NT_ - 1], l_recv)
    lane = lax.broadcasted_iota(i32, (NH, HD), 1)
    for half in range(2):
        picked = jnp.zeros((NH, HD), f32)
        for n in range(16):
            piece = plan[me_t * 32 + half * 16 + n]
            owner, local = piece // 32, lax.rem(piece, 32)
            tile = lall[owner, local // 16]
            shift = lax.rem(8 * n - 8 * lax.rem(local, 16) + HD, HD)
            picked = jnp.where(lane // 8 == n, pltpu.roll(tile, shift, 1), picked)
        ls_out[:, half * HD : (half + 1) * HD] = picked

    dv_out[...] = summed(1)
    dk_out[...] = summed(0)

    all_bytes(kv.at[NW - 1, :, : T - RB], z_send.at[0])
    all_bytes(qbuf.at[:, : T - RB], z_send.at[1])
    all_bytes(dobuf.at[:, : T - RB], z_send.at[2])
    all_bytes(kv.at[: NW - 1], w_send)
    all_bytes(lall.at[: NT_ - 1], l_send)
    all_bytes(gs_out, g_send.at[0])
    all_bytes(gy_out, g_send.at[1])
    all_bytes(gx_out, g_send.at[2])


def body(queries, key_rows, value_rows, out_grad, lengths, server_plan):
    any_spec = pl.BlockSpec(memory_space=pl.ANY)
    vmem = pl.BlockSpec(memory_space=pltpu.VMEM)
    smem = pl.BlockSpec(memory_space=pltpu.SMEM)
    dma, V = pltpu.SemaphoreType.DMA, pltpu.VMEM
    return pl.pallas_call(
        kernel,
        out_shape=[
            jax.ShapeDtypeStruct((T, NH * HD), bf16),
            jax.ShapeDtypeStruct((T, NH * HD), bf16),
            jax.ShapeDtypeStruct((T, HD), bf16),
            jax.ShapeDtypeStruct((T, HD), bf16),
            jax.ShapeDtypeStruct((NH, T), f32),
        ],
        in_specs=[any_spec] * 4 + [smem] * 2,
        out_specs=[vmem] * 5,
        scratch_shapes=[
            V((NCH, T, T), bf16),
            V((NCH, T, T), bf16),
            V((NW, 2, T, HD), bf16),
            V((T, HD), bf16),
            V((NW, T, HD), bf16),
            V((NH * T, NW * T), f32),
            V((NH * T, HD), f32),
            V((NH * T, NW * T), bf16),
            V((NH * T, HD), bf16),
            V((NH * T, HD), f32),
            V((T, HD), f32),
            V((2, NH, HD), f32),
            V((NT_, 2, NH, HD), f32),
            V((2, NW, HD, T), f32),
            V((2, 4, HD, T), bf16),
            V((2, 4, HD, T), bf16),
            V((2, 3, HD, T), bf16),
            V((2, 3, HD, T), bf16),
            V((2, HD, T), bf16),
            V((2, HD, T), bf16),
            dma((2 + 2 * NCH,)),
            dma((3,)),
            dma(()),
            dma((NCH,)),
            dma((NCH,)),
            dma(()),
            dma(()),
            dma((3,)),
            dma((4,)),
            dma(()),
            dma(()),
            dma((3,)),
            dma((2, 4)),
            dma((2, 3)),
            dma((2,)),
        ],
        compiler_params=pltpu.CompilerParams(
            collective_id=0, has_side_effects=True, vmem_limit_bytes=56 * 2**20
        ),
        cost_estimate=pl.CostEstimate(
            flops=8 * 10**9, bytes_accessed=6 * 2**20, transcendentals=5 * 10**6
        ),
        name="attention",
    )(queries, key_rows, value_rows, out_grad, lengths, server_plan)


def solution(mesh):
    in_specs = (
        P(("tok", "head"), None),
        P(("tok", "head"), None),
        P(("tok", "head"), None),
        P(("tok", "head"), None),
        P(),
        P(),
    )
    out_specs = (
        P("tok", "head"),
        P("tok", "head"),
        P("tok", "head"),
        P("tok", "head"),
        P("head", "tok"),
    )
    return jax.shard_map(body, mesh=mesh, in_specs=in_specs, out_specs=out_specs, check_vma=False)
```

```python
import functools

import jax
import jax.numpy as jnp
from jax import lax
from jax.experimental import pallas as pl
from jax.experimental.pallas import tpu as pltpu
from jax.sharding import PartitionSpec as P

bf16, f32, i32 = jnp.bfloat16, jnp.float32, jnp.int32
HD = 128
T = 256
NW = 9
NT_ = 32
NH = 8
RB = T // NH
NCH = 4
GR = 4 * T
NY = 4
NTRAJ = 8
SCALE = HD**-0.5
LOG2E = 1.4426950408889634
C = SCALE * LOG2E
BIG = 1e30
MESH = pl.DeviceIdType.MESH

NN, NT = ((1,), (0,)), ((1,), (1,))


def dot(a, b, dims):
    return lax.dot_general(a, b, (dims, ((), ())), preferred_element_type=f32)


def rows_of(buf, c):
    return jnp.concatenate([buf[c, :, :HD], buf[c, :, HD:]], axis=0)


def group_of(buf, g):
    return jnp.concatenate([rows_of(buf, 2 * g), rows_of(buf, 2 * g + 1)], axis=0)


def scores(w, c, qbuf, kv, maskq, maskk, s_all, mx):
    q = rows_of(qbuf, c)
    mask = maskq[...]
    qa = jnp.concatenate([q, jnp.concatenate([mask, mask], axis=0)], axis=1)
    ka = jnp.concatenate([kv[w, 0], maskk[w]], axis=1)
    s = dot(qa, ka, NT)
    if w == NW - 1:
        r = lax.rem(lax.broadcasted_iota(i32, s.shape, 0), T)
        s = jnp.where(lax.broadcasted_iota(i32, s.shape, 1) <= r, s, -BIG)
    at = slice(c * 2 * T, (c + 1) * 2 * T)
    s_all[at, w * T : (w + 1) * T] = s
    m = jnp.maximum(s[:, :HD], s[:, HD:])
    mx[at] = m if w == NW - 1 else jnp.maximum(mx[at], m)


def softmax(at, kv, s_all, mx, p_all):
    m = jnp.max(mx[at], axis=1, keepdims=True) * C
    acc = jnp.zeros((GR, 2 * HD), f32)
    ones = jnp.ones((T, HD), bf16)
    for w in range(NW):
        p = jnp.exp2(s_all[at, w * T : (w + 1) * T] * C - m).astype(bf16)
        p_all[at, w * T : (w + 1) * T] = p
        acc = acc + dot(p, jnp.concatenate([kv[w, 1], ones], axis=1), NN)
    l = acc[:, HD:]
    li = 1.0 / l
    return (acc[:, :HD] * li).astype(bf16), li, m * (1.0 / LOG2E) + jnp.log(l)


def with_out_dot(do, att):
    neg = -jnp.sum(do.astype(f32) * att.astype(f32), axis=1, keepdims=True)
    d1 = neg.astype(bf16).astype(f32)
    d2 = (neg - d1).astype(bf16).astype(f32)
    d3 = neg - d1 - d2
    lane = lax.broadcasted_iota(i32, do.shape, 1)
    ext = jnp.where(
        lane == 0, d1, jnp.where(lane == 1, d2, jnp.where(lane == 2, d3, 0.0))
    ).astype(bf16)
    return jnp.concatenate([do, ext], axis=1)


def kernel(
    q_in, k_in, v_in, do_in, lengths, plan,
    att_out, dq_out, dk_out, dv_out, ls_out,
    qbuf, dobuf, kv, maskq, maskk, s_all, mx, p_all, att, linv, lcol, lall, dkv_t,
    gs_out, gs_in, gd_out, gd_in,
    own_sem, z_send, kv_recv, q_recv, do_recv, w_send, wd_recv, ws_recv, l_send, l_recv,
    g_send, gs_recv, gd_recv,
):
    me_t, me_h = lax.axis_index("tok"), lax.axis_index("head")

    core = lax.rem(me_t, 2)
    y = lax.rem(me_t // 2, NY)
    sibling = (me_t + 1 - 2 * core, me_h)

    def y_peer(d):
        return (me_t + 2 * (lax.rem(y + d, NY) - y), me_h)

    def chip_peer(d):
        return (lax.rem(me_t + NT_ + 2 * d, NT_), me_h)

    def x_peer(d):
        return (lax.rem(me_t + 2 * NY * d, NT_), me_h)

    def head_peer(d):
        return (me_t, lax.rem(me_h + d, NH))

    barrier = pltpu.get_barrier_semaphore()
    for d in range(1, NH):
        pl.semaphore_signal(barrier, inc=1, device_id=head_peer(d), device_id_type=MESH)

    for peer in [sibling] + [chip_peer(d) for d in (1, 2, 3, 4, 8, -4, -3, -2, -1)]:
        pl.semaphore_signal(barrier, inc=1, device_id=peer, device_id_type=MESH)
    pl.semaphore_wait(barrier, NH - 1 + 10)

    rows = pl.ds(pl.multiple_of(me_h * RB, RB), RB)

    def remote(src, dst, send, recv, peer):
        return pltpu.make_async_remote_copy(
            src_ref=src, dst_ref=dst, send_sem=send, recv_sem=recv,
            device_id=peer, device_id_type=MESH,
        )

    def z_sends(d):
        h = lax.rem(me_h + d, NH)
        peer = (me_t, h)
        cols = pl.ds(pl.multiple_of(h * HD, HD), HD)
        remote(k_in.at[:, cols], kv.at[NW - 1, 0, rows], z_send.at[0], kv_recv, peer).start()
        remote(v_in.at[:, cols], kv.at[NW - 1, 1, rows], z_send.at[0], kv_recv, peer).start()

    def big_send(c, src, buf, send, recv):
        for d in range(1, NH):
            h = lax.rem(me_h + d, NH)
            cols = pl.ds(pl.multiple_of(h * NH * HD + c * T, T), T)
            remote(src.at[:, cols], buf.at[c, rows], send, recv.at[c], (me_t, h)).start()

    def q_send(c):
        big_send(c, q_in, qbuf, z_send.at[1], q_recv)

    def do_send(c):
        big_send(c, do_in, dobuf, z_send.at[2], do_recv)

    for d in range(1, NH):
        z_sends(d)
    q_send(0)
    q_send(1)

    own_cols = pl.ds(pl.multiple_of(me_h * HD, HD), HD)
    own = [
        (k_in.at[:, own_cols], kv.at[NW - 1, 0, rows]),
        (v_in.at[:, own_cols], kv.at[NW - 1, 1, rows]),
    ]
    for c in range(NCH):
        cols = pl.ds(pl.multiple_of(me_h * NH * HD + c * T, T), T)
        own.append((q_in.at[:, cols], qbuf.at[c, rows]))
        own.append((do_in.at[:, cols], dobuf.at[c, rows]))
    own = [pltpu.make_async_copy(s, t, own_sem.at[i]) for i, (s, t) in enumerate(own)]
    for copy in own:
        copy.start()

    lane = lax.broadcasted_iota(i32, (1, HD), 1)
    first = jnp.zeros((1, HD), i32)
    last = jnp.zeros((1, HD), i32)
    run = jnp.int32(0)
    for n in range(NTRAJ):
        first = jnp.where(lane == n, run, first)
        run = run + lengths[n]
        last = jnp.where(lane == n, run, last)
    row = lax.broadcasted_iota(i32, (T, HD), 0)
    for w in range(NW):
        pos = row + (me_t + w - (NW - 1)) * T
        inside = (pos >= first) & (pos < last)
        maskk[w] = jnp.where(inside, 0.0, 1.0).astype(bf16)
        if w == NW - 1:
            maskq[...] = jnp.where(inside, -BIG, 0.0).astype(bf16)
    lcol[...] = jnp.zeros((T, HD), f32)

    def all_bytes(ref, sem):
        pltpu.make_async_copy(ref, ref, sem).wait()

    for copy in own:
        copy.wait()
    all_bytes(kv.at[NW - 1, :, : T - RB], kv_recv)

    def window(src, dst, recv, peer):
        remote(kv.at[src], kv.at[dst], w_send, recv, peer).start()

    def share(d):
        i = d - core
        window(8 - 2 * d, 7 - 2 * i, ws_recv.at[i], sibling)

    for d in range(1, 5):
        window(8, 8 - 2 * d, wd_recv.at[d - 1], chip_peer(d))
    pl.when(core == 0)(lambda: share(0))
    q_send(2)
    q_send(3)

    def own_scores(c):
        all_bytes(qbuf.at[c, : T - RB], q_recv.at[c])
        scores(NW - 1, c, qbuf, kv, maskq, maskk, s_all, mx)

    own_scores(0)
    own_scores(1)
    do_send(0)
    do_send(1)
    for d in range(1, 5):
        all_bytes(kv.at[8 - 2 * d], wd_recv.at[d - 1])
        if d < 3:
            do_send(d + 1)
        if d < 4:
            share(d)
        else:
            pl.when(core == 1)(lambda: share(4))
    own_scores(2)
    own_scores(3)
    for w in (0, 6, 4, 2, 7, 5, 3, 1):
        if w % 2:
            all_bytes(kv.at[w], ws_recv.at[(7 - w) // 2])
        for c in range(NCH):
            scores(w, c, qbuf, kv, maskq, maskk, s_all, mx)

    @pl.loop(0, 2)
    def _(g):
        at = pl.ds(pl.multiple_of(g * GR, GR), GR)
        out, li, ls = softmax(at, kv, s_all, mx, p_all)
        att[at] = out
        linv[at] = li
        lanes = lax.broadcasted_iota(i32, (T, HD), 1)
        col = lcol[...]
        for i in range(4):
            col = jnp.where(lanes == 4 * g + i, ls[i * T : (i + 1) * T], col)
            att_out[:, pl.ds(pl.multiple_of((4 * g + i) * HD, HD), HD)] = out[i * T : (i + 1) * T]
        lcol[...] = col

    flat = lcol[...].T[:NH]
    mine = core * 16 + y * 4 + me_t // 8
    lall[mine, 0] = flat[:, :HD]
    lall[mine, 1] = flat[:, HD:]

    def l_share(index, count, recv, peer):
        part = lall.at[pl.ds(index, count)]
        remote(part, part, l_send, recv, peer).start()

    for d in (1, 2, 3):
        l_share(mine, 1, l_recv.at[d], x_peer(d))

    def l_over_y():
        for d in (1, 2, 3):
            all_bytes(lall.at[:1], l_recv.at[d])
        for d in (1, 2, 3):
            l_share(core * 16 + y * 4, 4, l_recv.at[3 + d], y_peer(d))

    def l_over_cores():
        for d in (1, 2, 3):
            all_bytes(lall.at[:4], l_recv.at[3 + d])
        l_share(core * 16, 16, l_recv.at[0], sibling)

    def sib_send(p, i):
        gs_out[p, i] = dkv_t[p, 7 - 2 * i].astype(bf16)
        remote(gs_out.at[p, i], gs_in.at[p, i], g_send.at[0], gs_recv.at[p, i], sibling).start()

    def only(cond, ref):
        return jnp.where(cond, ref.astype(f32), 0.0)

    def from_sibling(p, i):
        all_bytes(gs_in.at[p, i], gs_recv.at[p, i])
        return gs_in[p, i]

    def owner_send(p, d):
        i = d - core if d < 4 else 3 * core
        part = from_sibling(p, i)
        part = part.astype(f32) if d < 4 else only(core == 1, part)
        gd_out[p, d - 1] = (dkv_t[p, 8 - 2 * d] + part).astype(bf16)
        remote(
            gd_out.at[p, d - 1], gd_in.at[p, d - 1], g_send.at[1], gd_recv.at[p, d - 1], chip_peer(-d)
        ).start()

    def summed(p):
        total = dkv_t[p, 8] + only(core == 0, gs_in[p, 3 * core])
        for d in range(1, 5):
            all_bytes(gd_in.at[p, d - 1], gd_recv.at[p, d - 1])
            total = total + gd_in[p, d - 1].astype(f32)
        return total.T.astype(bf16)

    order = (7, 5, 3, 1, 6, 4, 2, 0, 8)
    ones = jnp.ones((T, HD), bf16)
    for g in range(2):
        at = slice(g * GR, (g + 1) * GR)
        for c in (2 * g, 2 * g + 1):
            all_bytes(dobuf.at[c, : T - RB], do_recv.at[c])
        do_t = (group_of(dobuf, g).astype(f32) * linv[at]).astype(bf16).T
        for w in order:
            dv = dot(do_t, p_all[at, w * T : (w + 1) * T], NN)
            if g == 0:
                dkv_t[1, w] = dv
            else:
                dkv_t[1, w] += dv
                if w % 2:
                    sib_send(1, (7 - w) // 2)
    l_over_y()
    for g in range(2):
        at = slice(g * GR, (g + 1) * GR)
        li = linv[at]
        q_t = (group_of(qbuf, g).astype(f32) * li * SCALE).astype(bf16).T
        doa = with_out_dot(group_of(dobuf, g), att[at])
        if g == 0:
            for d in range(1, 5):
                owner_send(1, d)
        acc = jnp.zeros((GR, HD), f32)
        for w in order:
            p = p_all[at, w * T : (w + 1) * T]
            va = jnp.concatenate([kv[w, 1], ones], axis=1)
            ds = (p.astype(f32) * dot(doa, va, NT)).astype(bf16)
            acc = acc + dot(ds, kv[w, 0], NN)
            dk = dot(q_t, ds, NN)
            if g == 0:
                dkv_t[0, w] = dk
            else:
                dkv_t[0, w] += dk
                if w % 2:
                    sib_send(0, (7 - w) // 2)
                elif w < 8:
                    owner_send(0, (8 - w) // 2)
        if g == 0:
            l_over_cores()
        dq = (acc * li * SCALE).astype(bf16)
        for i in range(4):
            dq_out[:, (4 * g + i) * HD : (4 * g + i + 1) * HD] = dq[i * T : (i + 1) * T]

    all_bytes(lall.at[:16], l_recv.at[0])
    lane = lax.broadcasted_iota(i32, (NH, HD), 1)
    for half in range(2):
        picked = jnp.zeros((NH, HD), f32)
        for n in range(16):
            piece = plan[me_t * 32 + half * 16 + n]
            owner, local = piece // 32, lax.rem(piece, 32)
            owner = lax.rem(owner, 2) * 16 + lax.rem(owner // 2, 4) * 4 + owner // 8
            tile = lall[owner, local // 16]
            shift = lax.rem(8 * n - 8 * lax.rem(local, 16) + HD, HD)
            picked = jnp.where(lane // 8 == n, pltpu.roll(tile, shift, 1), picked)
        ls_out[:, half * HD : (half + 1) * HD] = picked

    dv_out[...] = summed(1)
    dk_out[...] = summed(0)

    all_bytes(kv.at[NW - 1, :, : T - RB], z_send.at[0])
    all_bytes(qbuf.at[:, : T - RB], z_send.at[1])
    all_bytes(dobuf.at[:, : T - RB], z_send.at[2])
    all_bytes(kv.at[: NW - 1], w_send)
    all_bytes(lall.at[: 3 + 12 + 16], l_send)
    all_bytes(gs_out, g_send.at[0])
    all_bytes(gd_out, g_send.at[1])


def hand_over(*refs):
    sems = refs[-1]
    copies = [pltpu.make_async_copy(refs[i], refs[5 + i], sems.at[i]) for i in range(5)]
    for copy in copies:
        copy.start()
    for copy in copies:
        copy.wait()


def body(queries, key_rows, value_rows, out_grad, lengths, server_plan):
    any_spec = pl.BlockSpec(memory_space=pl.ANY)
    vmem = pl.BlockSpec(memory_space=pltpu.VMEM)
    smem = pl.BlockSpec(memory_space=pltpu.SMEM)
    dma, V = pltpu.SemaphoreType.DMA, pltpu.VMEM
    outs = pl.pallas_call(
        kernel,
        out_shape=[
            jax.ShapeDtypeStruct((T, NH * HD), bf16),
            jax.ShapeDtypeStruct((T, NH * HD), bf16),
            jax.ShapeDtypeStruct((T, HD), bf16),
            jax.ShapeDtypeStruct((T, HD), bf16),
            jax.ShapeDtypeStruct((NH, T), f32),
        ],
        in_specs=[any_spec] * 4 + [smem] * 2,
        out_specs=[vmem] * 5,
        scratch_shapes=[
            V((NCH, T, T), bf16),
            V((NCH, T, T), bf16),
            V((NW, 2, T, HD), bf16),
            V((T, HD), bf16),
            V((NW, T, HD), bf16),
            V((NH * T, NW * T), f32),
            V((NH * T, HD), f32),
            V((NH * T, NW * T), bf16),
            V((NH * T, HD), bf16),
            V((NH * T, HD), f32),
            V((T, HD), f32),
            V((NT_, 2, NH, HD), f32),
            V((2, NW, HD, T), f32),
            V((2, 4, HD, T), bf16),
            V((2, 4, HD, T), bf16),
            V((2, 4, HD, T), bf16),
            V((2, 4, HD, T), bf16),
            dma((2 + 2 * NCH,)),
            dma((3,)),
            dma(()),
            dma((NCH,)),
            dma((NCH,)),
            dma(()),
            dma((4,)),
            dma((4,)),
            dma(()),
            dma((7,)),
            dma((2,)),
            dma((2, 4)),
            dma((2, 4)),
        ],
        compiler_params=pltpu.CompilerParams(
            collective_id=0, has_side_effects=True, vmem_limit_bytes=56 * 2**20
        ),
        cost_estimate=pl.CostEstimate(
            flops=8 * 10**9, bytes_accessed=6 * 2**20, transcendentals=5 * 10**6
        ),
        name="attention",
    )(queries, key_rows, value_rows, out_grad, lengths, server_plan)
    return pl.pallas_call(
        hand_over,
        out_shape=[jax.ShapeDtypeStruct(a.shape, a.dtype) for a in outs],
        in_specs=[vmem] * 5,
        out_specs=[any_spec] * 5,
        scratch_shapes=[dma((5,))],
        name="hand_over",
    )(*outs)


def solution(mesh):
    in_specs = (
        P(("tok", "head"), None),
        P(("tok", "head"), None),
        P(("tok", "head"), None),
        P(("tok", "head"), None),
        P(),
        P(),
    )
    out_specs = (
        P("tok", "head"),
        P("tok", "head"),
        P("tok", "head"),
        P("tok", "head"),
        P("head", "tok"),
    )
    return jax.shard_map(body, mesh=mesh, in_specs=in_specs, out_specs=out_specs, check_vma=False)
```

```python
import functools

import jax
import jax.numpy as jnp
from jax import lax
from jax.experimental import pallas as pl
from jax.experimental.pallas import tpu as pltpu
from jax.sharding import PartitionSpec as P

bf16, f32, i32 = jnp.bfloat16, jnp.float32, jnp.int32
HD = 128
T = 256
NW = 9
NT_ = 32
NH = 8
RB = T // NH
NCH = 4
GR = 4 * T
NY = 4
NTRAJ = 8
SCALE = HD**-0.5
LOG2E = 1.4426950408889634
C = SCALE * LOG2E
BIG = 1e30
MESH = pl.DeviceIdType.MESH

NN, NT = ((1,), (0,)), ((1,), (1,))


def dot(a, b, dims):
    return lax.dot_general(a, b, (dims, ((), ())), preferred_element_type=f32)


def rows_of(buf, c):
    return jnp.concatenate([buf[c, :, :HD], buf[c, :, HD:]], axis=0)


def group_of(buf, g):
    return jnp.concatenate([rows_of(buf, 2 * g), rows_of(buf, 2 * g + 1)], axis=0)


def scores(w, c, qbuf, kv, maskq, maskk, s_all, mx):
    q = rows_of(qbuf, c)
    mask = maskq[...]
    qa = jnp.concatenate([q, jnp.concatenate([mask, mask], axis=0)], axis=1)
    ka = jnp.concatenate([kv[w, 0], maskk[w]], axis=1)
    s = dot(qa, ka, NT)
    if w == NW - 1:
        r = lax.rem(lax.broadcasted_iota(i32, s.shape, 0), T)
        s = jnp.where(lax.broadcasted_iota(i32, s.shape, 1) <= r, s, -BIG)
    at = slice(c * 2 * T, (c + 1) * 2 * T)
    s_all[at, w * T : (w + 1) * T] = s
    m = jnp.maximum(s[:, :HD], s[:, HD:])
    mx[at] = m if w == NW - 1 else jnp.maximum(mx[at], m)


def softmax(at, kv, s_all, mx, p_all):
    m = jnp.max(mx[at], axis=1, keepdims=True) * C
    acc = jnp.zeros((GR, 2 * HD), f32)
    ones = jnp.ones((T, HD), bf16)
    for w in range(NW):
        p = jnp.exp2(s_all[at, w * T : (w + 1) * T] * C - m).astype(bf16)
        p_all[at, w * T : (w + 1) * T] = p
        acc = acc + dot(p, jnp.concatenate([kv[w, 1], ones], axis=1), NN)
    l = acc[:, HD:]
    li = 1.0 / l
    return (acc[:, :HD] * li).astype(bf16), li, m * (1.0 / LOG2E) + jnp.log(l)


def with_out_dot(do, att):
    neg = -jnp.sum(do.astype(f32) * att.astype(f32), axis=1, keepdims=True)
    d1 = neg.astype(bf16).astype(f32)
    d2 = (neg - d1).astype(bf16).astype(f32)
    d3 = neg - d1 - d2
    lane = lax.broadcasted_iota(i32, do.shape, 1)
    ext = jnp.where(
        lane == 0, d1, jnp.where(lane == 1, d2, jnp.where(lane == 2, d3, 0.0))
    ).astype(bf16)
    return jnp.concatenate([do, ext], axis=1)


def kernel(
    q_in, k_in, v_in, do_in, lengths, plan,
    att_out, dq_out, dk_out, dv_out, ls_out,
    qbuf, dobuf, kv, maskq, maskk, s_all, mx, p_all, att, linv, lcol, lall, dkv_t,
    gs_out, gs_in, gd_out, gd_in,
    own_sem, z_send, kv_recv, q_recv, do_recv, w_send, wd_recv, ws_recv, l_send, l_recv,
    g_send, gs_recv, gd_recv,
):
    me_t, me_h = lax.axis_index("tok"), lax.axis_index("head")

    core = lax.rem(me_t, 2)
    y = lax.rem(me_t // 2, NY)
    sibling = (me_t + 1 - 2 * core, me_h)

    def y_peer(d):
        return (me_t + 2 * (lax.rem(y + d, NY) - y), me_h)

    def chip_peer(d):
        return (lax.rem(me_t + NT_ + 2 * d, NT_), me_h)

    def x_peer(d):
        return (lax.rem(me_t + 2 * NY * d, NT_), me_h)

    def head_peer(d):
        return (me_t, lax.rem(me_h + d, NH))

    barrier = pltpu.get_barrier_semaphore()
    for d in range(1, NH):
        pl.semaphore_signal(barrier, inc=1, device_id=head_peer(d), device_id_type=MESH)

    for peer in [sibling] + [chip_peer(d) for d in (1, 2, 3, 4, 8, -4, -3, -2, -1)]:
        pl.semaphore_signal(barrier, inc=1, device_id=peer, device_id_type=MESH)
    pl.semaphore_wait(barrier, NH - 1 + 10)

    rows = pl.ds(pl.multiple_of(me_h * RB, RB), RB)

    def remote(src, dst, send, recv, peer):
        return pltpu.make_async_remote_copy(
            src_ref=src, dst_ref=dst, send_sem=send, recv_sem=recv,
            device_id=peer, device_id_type=MESH,
        )

    def z_sends(d):
        h = lax.rem(me_h + d, NH)
        peer = (me_t, h)
        cols = pl.ds(pl.multiple_of(h * HD, HD), HD)
        remote(k_in.at[:, cols], kv.at[NW - 1, 0, rows], z_send.at[0], kv_recv, peer).start()
        remote(v_in.at[:, cols], kv.at[NW - 1, 1, rows], z_send.at[0], kv_recv, peer).start()

    def big_send(c, src, buf, send, recv):
        for d in range(1, NH):
            h = lax.rem(me_h + d, NH)
            cols = pl.ds(pl.multiple_of(h * NH * HD + c * T, T), T)
            remote(src.at[:, cols], buf.at[c, rows], send, recv.at[c], (me_t, h)).start()

    def q_send(c):
        big_send(c, q_in, qbuf, z_send.at[1], q_recv)

    def do_send(c):
        big_send(c, do_in, dobuf, z_send.at[2], do_recv)

    for d in range(1, NH):
        z_sends(d)
    q_send(0)
    q_send(1)

    own_cols = pl.ds(pl.multiple_of(me_h * HD, HD), HD)
    own = [
        (k_in.at[:, own_cols], kv.at[NW - 1, 0, rows]),
        (v_in.at[:, own_cols], kv.at[NW - 1, 1, rows]),
    ]
    for c in range(NCH):
        cols = pl.ds(pl.multiple_of(me_h * NH * HD + c * T, T), T)
        own.append((q_in.at[:, cols], qbuf.at[c, rows]))
        own.append((do_in.at[:, cols], dobuf.at[c, rows]))
    own = [pltpu.make_async_copy(s, t, own_sem.at[i]) for i, (s, t) in enumerate(own)]
    for copy in own:
        copy.start()

    lane = lax.broadcasted_iota(i32, (1, HD), 1)
    first = jnp.zeros((1, HD), i32)
    last = jnp.zeros((1, HD), i32)
    run = jnp.int32(0)
    for n in range(NTRAJ):
        first = jnp.where(lane == n, run, first)
        run = run + lengths[n]
        last = jnp.where(lane == n, run, last)
    row = lax.broadcasted_iota(i32, (T, HD), 0)
    for w in range(NW):
        pos = row + (me_t + w - (NW - 1)) * T
        inside = (pos >= first) & (pos < last)
        maskk[w] = jnp.where(inside, 0.0, 1.0).astype(bf16)
        if w == NW - 1:
            maskq[...] = jnp.where(inside, -BIG, 0.0).astype(bf16)
    lcol[...] = jnp.zeros((T, HD), f32)

    def all_bytes(ref, sem):
        pltpu.make_async_copy(ref, ref, sem).wait()

    for copy in own:
        copy.wait()
    all_bytes(kv.at[NW - 1, :, : T - RB], kv_recv)

    def window(src, dst, recv, peer):
        remote(kv.at[src], kv.at[dst], w_send, recv, peer).start()

    def share(d):
        i = d - core
        window(8 - 2 * d, 7 - 2 * i, ws_recv.at[i], sibling)

    for d in range(1, 5):
        window(8, 8 - 2 * d, wd_recv.at[d - 1], chip_peer(d))
    pl.when(core == 0)(lambda: share(0))
    q_send(2)
    q_send(3)

    def own_scores(c):
        all_bytes(qbuf.at[c, : T - RB], q_recv.at[c])
        scores(NW - 1, c, qbuf, kv, maskq, maskk, s_all, mx)

    own_scores(0)
    own_scores(1)
    do_send(0)
    do_send(1)
    for d in range(1, 5):
        all_bytes(kv.at[8 - 2 * d], wd_recv.at[d - 1])
        if d < 3:
            do_send(d + 1)
        if d < 4:
            share(d)
        else:
            pl.when(core == 1)(lambda: share(4))
    own_scores(2)
    own_scores(3)
    for w in (0, 6, 4, 2, 7, 5, 3, 1):
        if w % 2:
            all_bytes(kv.at[w], ws_recv.at[(7 - w) // 2])
        for c in range(NCH):
            scores(w, c, qbuf, kv, maskq, maskk, s_all, mx)

    @pl.loop(0, 2)
    def _(g):
        at = pl.ds(pl.multiple_of(g * GR, GR), GR)
        out, li, ls = softmax(at, kv, s_all, mx, p_all)
        att[at] = out
        linv[at] = li
        lanes = lax.broadcasted_iota(i32, (T, HD), 1)
        col = lcol[...]
        for i in range(4):
            col = jnp.where(lanes == 4 * g + i, ls[i * T : (i + 1) * T], col)
            att_out[:, pl.ds(pl.multiple_of((4 * g + i) * HD, HD), HD)] = out[i * T : (i + 1) * T]
        lcol[...] = col

    flat = lcol[...].T[:NH]
    mine = core * 16 + y * 4 + me_t // 8
    lall[mine, 0] = flat[:, :HD]
    lall[mine, 1] = flat[:, HD:]

    def l_share(index, count, recv, peer):
        part = lall.at[pl.ds(index, count)]
        remote(part, part, l_send, recv, peer).start()

    for d in (1, 2, 3):
        l_share(mine, 1, l_recv.at[d], x_peer(d))

    def l_over_y():
        for d in (1, 2, 3):
            all_bytes(lall.at[:1], l_recv.at[d])
        for d in (1, 2, 3):
            l_share(core * 16 + y * 4, 4, l_recv.at[3 + d], y_peer(d))

    def l_over_cores():
        for d in (1, 2, 3):
            all_bytes(lall.at[:4], l_recv.at[3 + d])
        l_share(core * 16, 16, l_recv.at[0], sibling)

    def sib_send(p, i):
        gs_out[p, i] = dkv_t[p, 7 - 2 * i].astype(bf16)
        remote(gs_out.at[p, i], gs_in.at[p, i], g_send.at[0], gs_recv.at[p, i], sibling).start()

    def add_sibling(p, w, i):
        all_bytes(gs_in.at[p, i], gs_recv.at[p, i])
        dkv_t[p, w] += gs_in[p, i].astype(f32)

    def owner_send(p, d):
        if d < 4:
            add_sibling(p, 8 - 2 * d, d - core)
        else:
            pl.when(core == 1)(lambda: add_sibling(p, 0, 3))
        gd_out[p, d - 1] = dkv_t[p, 8 - 2 * d].astype(bf16)
        remote(
            gd_out.at[p, d - 1], gd_in.at[p, d - 1], g_send.at[1], gd_recv.at[p, d - 1], chip_peer(-d)
        ).start()

    def summed(p):
        pl.when(core == 0)(lambda: add_sibling(p, 8, 0))
        total = dkv_t[p, 8]
        for d in range(4, 0, -1):
            all_bytes(gd_in.at[p, d - 1], gd_recv.at[p, d - 1])
            total = total + gd_in[p, d - 1].astype(f32)
        return total.T.astype(bf16)

    order = (1, 3, 5, 7, 0, 2, 4, 6, 8)
    ones = jnp.ones((T, HD), bf16)
    for g in range(2):
        at = slice(g * GR, (g + 1) * GR)
        for c in (2 * g, 2 * g + 1):
            all_bytes(dobuf.at[c, : T - RB], do_recv.at[c])
        do_t = (group_of(dobuf, g).astype(f32) * linv[at]).astype(bf16).T
        for w in order:
            dv = dot(do_t, p_all[at, w * T : (w + 1) * T], NN)
            if g == 0:
                dkv_t[1, w] = dv
            else:
                dkv_t[1, w] += dv
                if w % 2:
                    sib_send(1, (7 - w) // 2)
        if g == 0:
            l_over_y()
        li = linv[at]
        q_t = (group_of(qbuf, g).astype(f32) * li * SCALE).astype(bf16).T
        doa = with_out_dot(group_of(dobuf, g), att[at])
        acc = jnp.zeros((GR, HD), f32)
        for w in order:
            p = p_all[at, w * T : (w + 1) * T]
            va = jnp.concatenate([kv[w, 1], ones], axis=1)
            ds = (p.astype(f32) * dot(doa, va, NT)).astype(bf16)
            acc = acc + dot(ds, kv[w, 0], NN)
            dk = dot(q_t, ds, NN)
            if g == 0:
                dkv_t[0, w] = dk
            else:
                dkv_t[0, w] += dk
                if w % 2:
                    sib_send(0, (7 - w) // 2)
                elif w < 8:
                    owner_send(0, (8 - w) // 2)
                if w == 5:
                    for d in range(4, 0, -1):
                        owner_send(1, d)
        if g == 0:
            l_over_cores()
        dq = (acc * li * SCALE).astype(bf16)
        for i in range(4):
            dq_out[:, (4 * g + i) * HD : (4 * g + i + 1) * HD] = dq[i * T : (i + 1) * T]

    all_bytes(lall.at[:16], l_recv.at[0])
    lane = lax.broadcasted_iota(i32, (NH, HD), 1)
    for half in range(2):
        picked = jnp.zeros((NH, HD), f32)
        for n in range(16):
            piece = plan[me_t * 32 + half * 16 + n]
            owner, local = piece // 32, lax.rem(piece, 32)
            owner = lax.rem(owner, 2) * 16 + lax.rem(owner // 2, 4) * 4 + owner // 8
            tile = lall[owner, local // 16]
            shift = lax.rem(8 * n - 8 * lax.rem(local, 16) + HD, HD)
            picked = jnp.where(lane // 8 == n, pltpu.roll(tile, shift, 1), picked)
        ls_out[:, half * HD : (half + 1) * HD] = picked

    dv_out[...] = summed(1)
    dk_out[...] = summed(0)

    all_bytes(kv.at[NW - 1, :, : T - RB], z_send.at[0])
    all_bytes(qbuf.at[:, : T - RB], z_send.at[1])
    all_bytes(dobuf.at[:, : T - RB], z_send.at[2])
    all_bytes(kv.at[: NW - 1], w_send)
    all_bytes(lall.at[: 3 + 12 + 16], l_send)
    all_bytes(gs_out, g_send.at[0])
    all_bytes(gd_out, g_send.at[1])


def hand_over(*refs):
    sems = refs[-1]
    copies = [pltpu.make_async_copy(refs[i], refs[5 + i], sems.at[i]) for i in range(5)]
    for copy in copies:
        copy.start()
    for copy in copies:
        copy.wait()


def body(queries, key_rows, value_rows, out_grad, lengths, server_plan):
    any_spec = pl.BlockSpec(memory_space=pl.ANY)
    vmem = pl.BlockSpec(memory_space=pltpu.VMEM)
    smem = pl.BlockSpec(memory_space=pltpu.SMEM)
    dma, V = pltpu.SemaphoreType.DMA, pltpu.VMEM
    outs = pl.pallas_call(
        kernel,
        out_shape=[
            pltpu.VMEM((T, NH * HD), bf16),
            pltpu.VMEM((T, NH * HD), bf16),
            pltpu.VMEM((T, HD), bf16),
            pltpu.VMEM((T, HD), bf16),
            pltpu.VMEM((NH, T), f32),
        ],
        in_specs=[any_spec] * 4 + [smem] * 2,
        out_specs=[vmem] * 5,
        scratch_shapes=[
            V((NCH, T, T), bf16),
            V((NCH, T, T), bf16),
            V((NW, 2, T, HD), bf16),
            V((T, HD), bf16),
            V((NW, T, HD), bf16),
            V((NH * T, NW * T), f32),
            V((NH * T, HD), f32),
            V((NH * T, NW * T), bf16),
            V((NH * T, HD), bf16),
            V((NH * T, HD), f32),
            V((T, HD), f32),
            V((NT_, 2, NH, HD), f32),
            V((2, NW, HD, T), f32),
            V((2, 4, HD, T), bf16),
            V((2, 4, HD, T), bf16),
            V((2, 4, HD, T), bf16),
            V((2, 4, HD, T), bf16),
            dma((2 + 2 * NCH,)),
            dma((3,)),
            dma(()),
            dma((NCH,)),
            dma((NCH,)),
            dma(()),
            dma((4,)),
            dma((4,)),
            dma(()),
            dma((7,)),
            dma((2,)),
            dma((2, 4)),
            dma((2, 4)),
        ],
        compiler_params=pltpu.CompilerParams(
            collective_id=0, has_side_effects=True, vmem_limit_bytes=56 * 2**20
        ),
        cost_estimate=pl.CostEstimate(
            flops=8 * 10**9, bytes_accessed=6 * 2**20, transcendentals=5 * 10**6
        ),
        name="attention",
    )(queries, key_rows, value_rows, out_grad, lengths, server_plan)
    return pl.pallas_call(
        hand_over,
        out_shape=[jax.ShapeDtypeStruct(a.shape, a.dtype) for a in outs],
        in_specs=[vmem] * 5,
        out_specs=[any_spec] * 5,
        scratch_shapes=[dma((5,))],
        name="hand_over",
    )(*outs)


def solution(mesh):
    in_specs = (
        P(("tok", "head"), None),
        P(("tok", "head"), None),
        P(("tok", "head"), None),
        P(("tok", "head"), None),
        P(),
        P(),
    )
    out_specs = (
        P("tok", "head"),
        P("tok", "head"),
        P("tok", "head"),
        P("tok", "head"),
        P("head", "tok"),
    )
    return jax.shard_map(body, mesh=mesh, in_specs=in_specs, out_specs=out_specs, check_vma=False)
```

```python
import functools

import jax
import jax.numpy as jnp
from jax import lax
from jax.experimental import pallas as pl
from jax.experimental.pallas import tpu as pltpu
from jax.sharding import PartitionSpec as P

bf16, f32, i32 = jnp.bfloat16, jnp.float32, jnp.int32
HD = 128
T = 256
NW = 9
NT_ = 32
NH = 8
RB = T // NH
NCH = 4
GR = 4 * T
NY = 4
NTRAJ = 8
SCALE = HD**-0.5
LOG2E = 1.4426950408889634
C = SCALE * LOG2E
BIG = 1e30
MESH = pl.DeviceIdType.MESH

NN, NT = ((1,), (0,)), ((1,), (1,))


def dot(a, b, dims):
    return lax.dot_general(a, b, (dims, ((), ())), preferred_element_type=f32)


def rows_of(buf, c):
    return jnp.concatenate([buf[c, :, :HD], buf[c, :, HD:]], axis=0)


def group_of(buf, g):
    return jnp.concatenate([rows_of(buf, 2 * g), rows_of(buf, 2 * g + 1)], axis=0)


def scores(w, c, qbuf, kv, maskq, maskk, s_all, mx):
    q = rows_of(qbuf, c)
    mask = maskq[...]
    qa = jnp.concatenate([q, jnp.concatenate([mask, mask], axis=0)], axis=1)
    ka = jnp.concatenate([kv[w, 0], maskk[w]], axis=1)
    s = dot(qa, ka, NT)
    if w == NW - 1:
        r = lax.rem(lax.broadcasted_iota(i32, s.shape, 0), T)
        s = jnp.where(lax.broadcasted_iota(i32, s.shape, 1) <= r, s, -BIG)
    at = slice(c * 2 * T, (c + 1) * 2 * T)
    s_all[at, w * T : (w + 1) * T] = s
    m = jnp.maximum(s[:, :HD], s[:, HD:])
    mx[at] = m if w == NW - 1 else jnp.maximum(mx[at], m)


def softmax(at, kv, s_all, mx, p_all):
    m = jnp.max(mx[at], axis=1, keepdims=True) * C
    acc = jnp.zeros((GR, 2 * HD), f32)
    ones = jnp.ones((T, HD), bf16)
    for w in range(NW):
        p = jnp.exp2(s_all[at, w * T : (w + 1) * T] * C - m).astype(bf16)
        p_all[at, w * T : (w + 1) * T] = p
        acc = acc + dot(p, jnp.concatenate([kv[w, 1], ones], axis=1), NN)
    l = acc[:, HD:]
    li = 1.0 / l
    return (acc[:, :HD] * li).astype(bf16), li, m * (1.0 / LOG2E) + jnp.log(l)


def with_out_dot(do, att):
    neg = -jnp.sum(do.astype(f32) * att.astype(f32), axis=1, keepdims=True)
    d1 = neg.astype(bf16).astype(f32)
    d2 = (neg - d1).astype(bf16).astype(f32)
    d3 = neg - d1 - d2
    lane = lax.broadcasted_iota(i32, do.shape, 1)
    ext = jnp.where(
        lane == 0, d1, jnp.where(lane == 1, d2, jnp.where(lane == 2, d3, 0.0))
    ).astype(bf16)
    return jnp.concatenate([do, ext], axis=1)


def kernel(
    q_in, k_in, v_in, do_in, lengths, plan,
    att_out, dq_out, dk_out, dv_out, ls_out,
    qbuf, dobuf, kv, maskq, maskk, s_all, mx, p_all, att, linv, lcol, lall, dkv_t,
    gs_out, gs_in, gd_out, gd_in,
    own_sem, z_send, kv_recv, q_recv, do_recv, w_send, wd_recv, ws_recv, l_send, l_recv,
    g_send, gs_recv, gd_recv,
):
    me_t, me_h = lax.axis_index("tok"), lax.axis_index("head")

    core = lax.rem(me_t, 2)
    y = lax.rem(me_t // 2, NY)
    sibling = (me_t + 1 - 2 * core, me_h)

    def y_peer(d):
        return (me_t + 2 * (lax.rem(y + d, NY) - y), me_h)

    def chip_peer(d):
        return (lax.rem(me_t + NT_ + 2 * d, NT_), me_h)

    def x_peer(d):
        return (lax.rem(me_t + 2 * NY * d, NT_), me_h)

    def head_peer(d):
        return (me_t, lax.rem(me_h + d, NH))

    barrier = pltpu.get_barrier_semaphore()
    for d in range(1, NH):
        pl.semaphore_signal(barrier, inc=1, device_id=head_peer(d), device_id_type=MESH)

    for peer in [sibling] + [chip_peer(d) for d in (1, 2, 3, 4, 8, -4, -3, -2, -1)]:
        pl.semaphore_signal(barrier, inc=1, device_id=peer, device_id_type=MESH)
    pl.semaphore_wait(barrier, NH - 1 + 10)

    rows = pl.ds(pl.multiple_of(me_h * RB, RB), RB)

    def remote(src, dst, send, recv, peer):
        return pltpu.make_async_remote_copy(
            src_ref=src, dst_ref=dst, send_sem=send, recv_sem=recv,
            device_id=peer, device_id_type=MESH,
        )

    def kv_send(part, src):
        for d in range(1, NH):
            h = lax.rem(me_h + d, NH)
            cols = pl.ds(pl.multiple_of(h * HD, HD), HD)
            dst = kv.at[NW - 1, part, rows]
            remote(src.at[:, cols], dst, z_send.at[0], kv_recv.at[part], (me_t, h)).start()

    def big_send(c, src, buf, send, recv):
        for d in range(1, NH):
            h = lax.rem(me_h + d, NH)
            cols = pl.ds(pl.multiple_of(h * NH * HD + c * T, T), T)
            remote(src.at[:, cols], buf.at[c, rows], send, recv.at[c], (me_t, h)).start()

    def q_send(c):
        big_send(c, q_in, qbuf, z_send.at[1], q_recv)

    def do_send(c):
        big_send(c, do_in, dobuf, z_send.at[2], do_recv)

    kv_send(0, k_in)
    kv_send(1, v_in)

    own_cols = pl.ds(pl.multiple_of(me_h * HD, HD), HD)
    own = [
        (k_in.at[:, own_cols], kv.at[NW - 1, 0, rows]),
        (v_in.at[:, own_cols], kv.at[NW - 1, 1, rows]),
    ]
    for c in range(NCH):
        cols = pl.ds(pl.multiple_of(me_h * NH * HD + c * T, T), T)
        own.append((q_in.at[:, cols], qbuf.at[c, rows]))
        own.append((do_in.at[:, cols], dobuf.at[c, rows]))
    own = [pltpu.make_async_copy(s, t, own_sem.at[i]) for i, (s, t) in enumerate(own)]
    for copy in own:
        copy.start()

    lane = lax.broadcasted_iota(i32, (1, HD), 1)
    first = jnp.zeros((1, HD), i32)
    last = jnp.zeros((1, HD), i32)
    run = jnp.int32(0)
    for n in range(NTRAJ):
        first = jnp.where(lane == n, run, first)
        run = run + lengths[n]
        last = jnp.where(lane == n, run, last)
    row = lax.broadcasted_iota(i32, (T, HD), 0)
    for w in range(NW):
        pos = row + (me_t + w - (NW - 1)) * T
        inside = (pos >= first) & (pos < last)
        maskk[w] = jnp.where(inside, 0.0, 1.0).astype(bf16)
        if w == NW - 1:
            maskq[...] = jnp.where(inside, -BIG, 0.0).astype(bf16)
    lcol[...] = jnp.zeros((T, HD), f32)
    q_send(0)
    q_send(1)

    def all_bytes(ref, sem):
        pltpu.make_async_copy(ref, ref, sem).wait()

    for copy in own:
        copy.wait()
    def window(part, src, dst, recv, peer):
        remote(kv.at[src, part], kv.at[dst, part], w_send, recv, peer).start()

    def share(part, d):
        i = d - core
        window(part, 8 - 2 * d, 7 - 2 * i, ws_recv.at[part, i], sibling)

    def spread(part):
        all_bytes(kv.at[NW - 1, part, : T - RB], kv_recv.at[part])
        for d in range(1, 5):
            window(part, 8, 8 - 2 * d, wd_recv.at[part, d - 1], chip_peer(d))
        pl.when(core == 0)(lambda: share(part, 0))

    def pass_across(part):
        for d in range(1, 5):
            all_bytes(kv.at[8 - 2 * d, part], wd_recv.at[part, d - 1])
            if d < 4:
                share(part, d)
            else:
                pl.when(core == 1)(lambda: share(part, 4))

    def own_scores(c):
        all_bytes(qbuf.at[c, : T - RB], q_recv.at[c])
        scores(NW - 1, c, qbuf, kv, maskq, maskk, s_all, mx)

    def soft(g):
        at = slice(g * GR, (g + 1) * GR)
        out, li, ls = softmax(at, kv, s_all, mx, p_all)
        att[at] = out
        linv[at] = li
        lanes = lax.broadcasted_iota(i32, (T, HD), 1)
        col = lcol[...]
        for i in range(4):
            j = 4 * g + i
            col = jnp.where(lanes == j, ls[i * T : (i + 1) * T], col)
            att_out[:, j * HD : (j + 1) * HD] = out[i * T : (i + 1) * T]
        lcol[...] = col

    spread(0)
    q_send(2)
    spread(1)
    q_send(3)
    own_scores(0)
    pass_across(0)
    do_send(0)
    own_scores(1)
    for w in (6, 4, 2, 0, 7, 5, 3, 1):
        if w % 2:
            all_bytes(kv.at[w, 0], ws_recv.at[0, (7 - w) // 2])
        for c in (0, 1):
            scores(w, c, qbuf, kv, maskq, maskk, s_all, mx)
    do_send(1)
    pass_across(1)
    do_send(2)
    for i in range(4):
        all_bytes(kv.at[7 - 2 * i, 1], ws_recv.at[1, i])
    soft(0)
    do_send(3)
    own_scores(2)
    own_scores(3)
    for w in (6, 4, 2, 0, 7, 5, 3, 1):
        for c in (2, 3):
            scores(w, c, qbuf, kv, maskq, maskk, s_all, mx)
    soft(1)

    flat = lcol[...].T[:NH]
    mine = core * 16 + y * 4 + me_t // 8
    lall[mine, 0] = flat[:, :HD]
    lall[mine, 1] = flat[:, HD:]

    def l_share(index, count, recv, peer):
        part = lall.at[pl.ds(index, count)]
        remote(part, part, l_send, recv, peer).start()

    for d in (1, 2, 3):
        l_share(mine, 1, l_recv.at[d], x_peer(d))

    def l_over_y():
        for d in (1, 2, 3):
            all_bytes(lall.at[:1], l_recv.at[d])
        for d in (1, 2, 3):
            l_share(core * 16 + y * 4, 4, l_recv.at[3 + d], y_peer(d))

    def l_over_cores():
        for d in (1, 2, 3):
            all_bytes(lall.at[:4], l_recv.at[3 + d])
        l_share(core * 16, 16, l_recv.at[0], sibling)

    def sib_send(p, i):
        gs_out[p, i] = dkv_t[p, 7 - 2 * i].astype(bf16)
        remote(gs_out.at[p, i], gs_in.at[p, i], g_send.at[0], gs_recv.at[p, i], sibling).start()

    def add_sibling(p, w, i):
        all_bytes(gs_in.at[p, i], gs_recv.at[p, i])
        dkv_t[p, w] += gs_in[p, i].astype(f32)

    def owner_send(p, d):
        if d < 4:
            add_sibling(p, 8 - 2 * d, d - core)
        else:
            pl.when(core == 1)(lambda: add_sibling(p, 0, 3))
        gd_out[p, d - 1] = dkv_t[p, 8 - 2 * d].astype(bf16)
        remote(
            gd_out.at[p, d - 1], gd_in.at[p, d - 1], g_send.at[1], gd_recv.at[p, d - 1], chip_peer(-d)
        ).start()

    def summed(p):
        pl.when(core == 0)(lambda: add_sibling(p, 8, 0))
        total = dkv_t[p, 8]
        for d in range(4, 0, -1):
            all_bytes(gd_in.at[p, d - 1], gd_recv.at[p, d - 1])
            total = total + gd_in[p, d - 1].astype(f32)
        return total.T.astype(bf16)

    order = (1, 3, 5, 7, 0, 2, 4, 6, 8)
    ones = jnp.ones((T, HD), bf16)
    for g in range(2):
        at = slice(g * GR, (g + 1) * GR)
        for c in (2 * g, 2 * g + 1):
            all_bytes(dobuf.at[c, : T - RB], do_recv.at[c])
        do_t = (group_of(dobuf, g).astype(f32) * linv[at]).astype(bf16).T
        for w in order:
            dv = dot(do_t, p_all[at, w * T : (w + 1) * T], NN)
            if g == 0:
                dkv_t[1, w] = dv
            else:
                dkv_t[1, w] += dv
                if w % 2:
                    sib_send(1, (7 - w) // 2)
        if g == 0:
            l_over_y()
        li = linv[at]
        q_t = (group_of(qbuf, g).astype(f32) * li * SCALE).astype(bf16).T
        doa = with_out_dot(group_of(dobuf, g), att[at])
        acc = jnp.zeros((GR, HD), f32)
        for w in order:
            p = p_all[at, w * T : (w + 1) * T]
            va = jnp.concatenate([kv[w, 1], ones], axis=1)
            ds = (p.astype(f32) * dot(doa, va, NT)).astype(bf16)
            acc = acc + dot(ds, kv[w, 0], NN)
            dk = dot(q_t, ds, NN)
            if g == 0:
                dkv_t[0, w] = dk
            else:
                dkv_t[0, w] += dk
                if w % 2:
                    sib_send(0, (7 - w) // 2)
                elif w < 8:
                    owner_send(0, (8 - w) // 2)
                if w == 5:
                    for d in range(4, 0, -1):
                        owner_send(1, d)
        if g == 0:
            l_over_cores()
        dq = (acc * li * SCALE).astype(bf16)
        for i in range(4):
            dq_out[:, (4 * g + i) * HD : (4 * g + i + 1) * HD] = dq[i * T : (i + 1) * T]

    all_bytes(lall.at[:16], l_recv.at[0])
    lane = lax.broadcasted_iota(i32, (NH, HD), 1)
    for half in range(2):
        picked = jnp.zeros((NH, HD), f32)
        for n in range(16):
            piece = plan[me_t * 32 + half * 16 + n]
            owner, local = piece // 32, lax.rem(piece, 32)
            owner = lax.rem(owner, 2) * 16 + lax.rem(owner // 2, 4) * 4 + owner // 8
            tile = lall[owner, local // 16]
            shift = lax.rem(8 * n - 8 * lax.rem(local, 16) + HD, HD)
            picked = jnp.where(lane // 8 == n, pltpu.roll(tile, shift, 1), picked)
        ls_out[:, half * HD : (half + 1) * HD] = picked

    dv_out[...] = summed(1)
    dk_out[...] = summed(0)

    all_bytes(kv.at[NW - 1, :, : T - RB], z_send.at[0])
    all_bytes(qbuf.at[:, : T - RB], z_send.at[1])
    all_bytes(dobuf.at[:, : T - RB], z_send.at[2])
    all_bytes(kv.at[: NW - 1], w_send)
    all_bytes(lall.at[: 3 + 12 + 16], l_send)
    all_bytes(gs_out, g_send.at[0])
    all_bytes(gd_out, g_send.at[1])


def hand_over(*refs):
    sems = refs[-1]
    copies = [pltpu.make_async_copy(refs[i], refs[5 + i], sems.at[i]) for i in range(5)]
    for copy in copies:
        copy.start()
    for copy in copies:
        copy.wait()


def body(queries, key_rows, value_rows, out_grad, lengths, server_plan):
    any_spec = pl.BlockSpec(memory_space=pl.ANY)
    vmem = pl.BlockSpec(memory_space=pltpu.VMEM)
    smem = pl.BlockSpec(memory_space=pltpu.SMEM)
    dma, V = pltpu.SemaphoreType.DMA, pltpu.VMEM
    outs = pl.pallas_call(
        kernel,
        out_shape=[
            jax.ShapeDtypeStruct((T, NH * HD), bf16),
            jax.ShapeDtypeStruct((T, NH * HD), bf16),
            jax.ShapeDtypeStruct((T, HD), bf16),
            jax.ShapeDtypeStruct((T, HD), bf16),
            jax.ShapeDtypeStruct((NH, T), f32),
        ],
        in_specs=[any_spec] * 4 + [smem] * 2,
        out_specs=[vmem] * 5,
        scratch_shapes=[
            V((NCH, T, T), bf16),
            V((NCH, T, T), bf16),
            V((NW, 2, T, HD), bf16),
            V((T, HD), bf16),
            V((NW, T, HD), bf16),
            V((NH * T, NW * T), f32),
            V((NH * T, HD), f32),
            V((NH * T, NW * T), bf16),
            V((NH * T, HD), bf16),
            V((NH * T, HD), f32),
            V((T, HD), f32),
            V((NT_, 2, NH, HD), f32),
            V((2, NW, HD, T), f32),
            V((2, 4, HD, T), bf16),
            V((2, 4, HD, T), bf16),
            V((2, 4, HD, T), bf16),
            V((2, 4, HD, T), bf16),
            dma((2 + 2 * NCH,)),
            dma((3,)),
            dma((2,)),
            dma((NCH,)),
            dma((NCH,)),
            dma(()),
            dma((2, 4)),
            dma((2, 4)),
            dma(()),
            dma((7,)),
            dma((2,)),
            dma((2, 4)),
            dma((2, 4)),
        ],
        compiler_params=pltpu.CompilerParams(
            collective_id=0, has_side_effects=True, vmem_limit_bytes=56 * 2**20
        ),
        cost_estimate=pl.CostEstimate(
            flops=8 * 10**9, bytes_accessed=6 * 2**20, transcendentals=5 * 10**6
        ),
        name="attention",
    )(queries, key_rows, value_rows, out_grad, lengths, server_plan)
    return pl.pallas_call(
        hand_over,
        out_shape=[jax.ShapeDtypeStruct(a.shape, a.dtype) for a in outs],
        in_specs=[vmem] * 5,
        out_specs=[any_spec] * 5,
        scratch_shapes=[dma((5,))],
        name="hand_over",
    )(*outs)


def solution(mesh):
    in_specs = (
        P(("tok", "head"), None),
        P(("tok", "head"), None),
        P(("tok", "head"), None),
        P(("tok", "head"), None),
        P(),
        P(),
    )
    out_specs = (
        P("tok", "head"),
        P("tok", "head"),
        P("tok", "head"),
        P("tok", "head"),
        P("head", "tok"),
    )
    return jax.shard_map(body, mesh=mesh, in_specs=in_specs, out_specs=out_specs, check_vma=False)
```
